512 devices in a mesh: fsdp: 64 (over z, y), tensor: 8 (over x, core).
Axes of the slice: x: 4, y: 4, z: 16, core: 2. Of those that a mesh axis runs over, the one named last changes fastest.
Arguments:
- grads: float32 [64, 1024, 1024], P(None, 'fsdp', 'tensor'), may hold values from -20 to 20
- block_slot: int32 [64], replicated, may hold values from 0 to 127, as said below
- stat_left: bfloat16 [128, 1024, 1024], P('fsdp', 'tensor'), may hold values from -6 to 6
- stat_right: bfloat16 [128, 1024, 1024], P('fsdp', 'tensor'), may hold values from -6 to 6
- root_left: bfloat16 [128, 1024, 1024], P('fsdp', 'tensor'), may hold values from -1 to 2
- root_right: bfloat16 [128, 1024, 1024], P('fsdp', None, 'tensor'), may hold values from -1 to 2
Outputs:
- directions: bfloat16 [64, 1024, 1024], P(None, 'fsdp', 'tensor')
- new_left: bfloat16 [128, 1024, 1024], P('fsdp', 'tensor')
- new_right: bfloat16 [128, 1024, 1024], P('fsdp', 'tensor')
The draws below stay inside these ranges and needn't reach their ends.
Inputs may be any that keep to these rules, and one draw needn't show every extreme that they name: `block_slot`: the slots are distinct; slot s belongs to owner s // 2 along fsdp; in every draw some owner has all its 2 slots taken.
All inputs are finite; a program needn't handle non-finite values.
Results may differ from the reference program's by a relative error of at most 0.0057.
Values may be sent and summed in bfloat16 or wider, within the bound.
A program may use at most 64 MiB of HBM per device.

```python
import math
import jax
import jax.numpy as jnp
from jax import lax

BLK = 1024
SLOTS = 2
BLOCKS = 64
SLOT_ALL = 128
N_FSDP = 64


def draw_grads(key, part):
    key = jax.random.fold_in(key, 1)
    key_base, key_rows, key_cols = jax.random.split(key, 3)
    row_scale = jnp.exp(jax.random.uniform(key_rows, (BLOCKS, BLK, 1), jnp.float32, math.log(0.5), math.log(5.0)))
    col_scale = jnp.exp(jax.random.uniform(key_cols, (BLOCKS, 1, BLK), jnp.float32, math.log(0.5), math.log(5.0)))
    column_ramp = jnp.power(3.0, jnp.arange(BLK, dtype=jnp.float32) / BLK)[None, None, :]
    base_part = jax.random.truncated_normal(key_base, -6.0, 6.0, (BLOCKS, BLK, BLK), jnp.float32)
    value = 0.03 * base_part * row_scale * col_scale * column_ramp
    return value.astype(jnp.float32)


def draw_block_slot(key, part):
    key = jax.random.fold_in(key, 2)
    key_owner, key_order, key_blocks = jax.random.split(key, 3)
    owner = jax.random.randint(key_owner, (), 0, N_FSDP)
    slot_ids = jnp.arange(SLOT_ALL, dtype=jnp.int32)
    scores = jax.random.permutation(key_order, SLOT_ALL).astype(jnp.int32) + SLOTS
    forced = slot_ids // SLOTS == owner
    scores = jnp.where(forced, slot_ids % SLOTS, scores)
    ordered = jnp.argsort(scores, stable=True).astype(jnp.int32)
    chosen = ordered[:BLOCKS]
    return jax.random.permutation(key_blocks, chosen).astype(jnp.int32)


def root_matrix(key):
    key_diag, key_noise = jax.random.split(key)
    diagonal = jax.random.uniform(key_diag, (SLOT_ALL, BLK, 1), jnp.float32, 0.6, 1.4)
    noise = jax.random.truncated_normal(key_noise, -6.0, 6.0, (SLOT_ALL, BLK, BLK), jnp.float32)
    identity = jnp.eye(BLK, dtype=jnp.float32)[None, :, :]
    return (identity * diagonal + noise * (0.35 / math.sqrt(BLK))).astype(jnp.bfloat16)


def draw_root_left(key, part):
    key = jax.random.fold_in(key, 3)
    return root_matrix(key)


def draw_root_right(key, part):
    key = jax.random.fold_in(key, 4)
    return root_matrix(key)


def block_scale(rng, shape, cuts, least, largest):
    def one(axis_at, shards_of):
        draws = jax.random.uniform(jax.random.fold_in(jax.random.fold_in(rng, 6), axis_at), (shards_of,), jnp.float32, least / len(cuts), largest / len(cuts))
        return jnp.repeat(jnp.exp(draws), shape[axis_at] // shards_of).reshape((-1,) + (1,) * (len(shape) - axis_at - 1))

    factor_of = one(*cuts[0])
    for cut in cuts[1:]:
        factor_of = factor_of * one(*cut)
    return factor_of


def bell_draw(stream_key, dims, spread, most, shards=(), held_as=jnp.bfloat16):
    array = jax.random.normal(stream_key, dims, jnp.float32) * spread
    if len(shards) > 0:
        array = block_scale(stream_key, dims, shards, -0.22, 0.18) * array
    return jnp.clip(array, min=-most, max=most).astype(held_as)


def setup_inputs(seed: int = 0) -> dict:
    key_of = jax.random.split(jax.random.key(seed), 7)
    grads = draw_grads(jax.random.fold_in(key_of[6], 71), 0)
    block_slot = draw_block_slot(jax.random.fold_in(key_of[6], 71), 0)
    stat_left = bell_draw(key_of[2], (SLOT_ALL, BLK, BLK), 1.0, 6.0, ((0, 64), (1, 8)))
    stat_right = bell_draw(key_of[3], (SLOT_ALL, BLK, BLK), 1.0, 6.0, ((0, 64), (1, 8)))
    root_left = draw_root_left(jax.random.fold_in(key_of[6], 71), 0)
    root_right = draw_root_right(jax.random.fold_in(key_of[6], 71), 0)
    return {"grads": grads, "block_slot": block_slot, "stat_left": stat_left, "stat_right": stat_right, "root_left": root_left, "root_right": root_right}


stat_decay = 0.95
graft_eps = 1e-06

def reference(grads, block_slot, stat_left, stat_right, root_left, root_right):

    def one_block(index):
        gradient = grads[index]
        slot = block_slot[index]
        left_prod = jnp.dot(gradient, gradient.T, precision=lax.Precision.HIGHEST)
        right_prod = jnp.dot(gradient.T, gradient, precision=lax.Precision.HIGHEST)
        left_b = (stat_decay * stat_left[slot].astype(jnp.float32) + (1.0 - stat_decay) * left_prod).astype(jnp.bfloat16)
        right_b = (stat_decay * stat_right[slot].astype(jnp.float32) + (1.0 - stat_decay) * right_prod).astype(jnp.bfloat16)
        half_right = jnp.dot(gradient.astype(jnp.bfloat16), root_right[slot], preferred_element_type=jnp.float32).astype(jnp.bfloat16)
        precond = jnp.dot(root_left[slot], half_right, preferred_element_type=jnp.float32)
        scale = jnp.sqrt(jnp.sum(gradient * gradient) / (jnp.sum(precond * precond) + graft_eps))
        return ((precond * scale).astype(jnp.bfloat16), left_b, right_b)
    directions, lefts, rights = lax.map(one_block, jnp.arange(BLOCKS, dtype=jnp.int32))
    new_left = stat_left.at[block_slot].set(lefts)
    new_right = stat_right.at[block_slot].set(rights)
    return (directions, new_left, new_right)
```

```python
import jax
import jax.numpy as jnp
from jax import lax
from jax.sharding import PartitionSpec as P

stat_decay = 0.95
graft_eps = 1e-06


def on_device(grads, block_slot, stat_left, stat_right, root_left, root_right):
    fsdp_count = lax.axis_size("fsdp")
    owner_index = lax.axis_index("fsdp")
    tensor_index = lax.axis_index("tensor")
    block_count, row_share, col_share = grads.shape
    slot_count = stat_left.shape[0]
    left_rows = stat_left.shape[1]
    slot_total = fsdp_count * slot_count
    slot_ids = jnp.arange(slot_total, dtype=jnp.int32)
    slot_match = block_slot[None, :] == slot_ids[:, None]
    slot_used = jnp.any(slot_match, axis=1)
    mine_used = lax.dynamic_index_in_dim(
        slot_used.reshape(fsdp_count, slot_count), owner_index, 0, keepdims=False
    )
    whole_root_left = lax.all_gather(root_left, "tensor", axis=1, tiled=True)
    picked = jnp.einsum(
        "sb,brc->src",
        slot_match.astype(jnp.bfloat16),
        grads.astype(jnp.bfloat16),
        preferred_element_type=jnp.float32,
    ).astype(jnp.bfloat16)
    col_slab = lax.all_to_all(
        picked.reshape(fsdp_count, slot_count, row_share, col_share),
        "fsdp",
        split_axis=0,
        concat_axis=2,
        tiled=True,
    )[0]
    full_block = lax.all_gather(col_slab, "tensor", axis=2, tiled=True)
    row_block = lax.dynamic_slice_in_dim(full_block, tensor_index * left_rows, left_rows, 1)
    left_prod = jnp.einsum("srk,sck->src", row_block, full_block, preferred_element_type=jnp.float32)
    right_prod = jnp.einsum("skr,skc->src", col_slab, full_block, preferred_element_type=jnp.float32)
    keep_mask = mine_used[:, None, None]
    left_old = stat_left.astype(jnp.float32)
    right_old = stat_right.astype(jnp.float32)
    new_left = jnp.where(
        keep_mask, stat_decay * left_old + (1.0 - stat_decay) * left_prod, left_old
    ).astype(jnp.bfloat16)
    new_right = jnp.where(
        keep_mask, stat_decay * right_old + (1.0 - stat_decay) * right_prod, right_old
    ).astype(jnp.bfloat16)
    half_right = jnp.einsum(
        "sik,skj->sij", full_block, root_right, preferred_element_type=jnp.float32
    ).astype(jnp.bfloat16)
    precond = jnp.einsum(
        "snk,skj->snj", whole_root_left, half_right, preferred_element_type=jnp.float32
    )
    slab_wide = col_slab.astype(jnp.float32)
    dir_part = jnp.sum(precond * precond, axis=(1, 2))
    grad_part = jnp.sum(slab_wide * slab_wide, axis=(1, 2))
    grad_sq, dir_sq = lax.psum((grad_part, dir_part), "tensor")
    graft_scale = jnp.sqrt(grad_sq / (dir_sq + graft_eps))
    direction = (precond * graft_scale[:, None, None]).astype(jnp.bfloat16)
    send_back = direction.reshape(slot_count, fsdp_count, row_share, col_share)
    returned = lax.all_to_all(send_back, "fsdp", split_axis=1, concat_axis=0, tiled=True)
    by_slot = returned.reshape(slot_total, row_share, col_share)
    directions = by_slot[block_slot]
    return (directions, new_left, new_right)


def solution(mesh):
    placed = (
        P(None, "fsdp", "tensor"),
        P(),
        P("fsdp", "tensor", None),
        P("fsdp", "tensor", None),
        P("fsdp", "tensor", None),
        P("fsdp", None, "tensor"),
    )
    return jax.shard_map(
        on_device,
        mesh=mesh,
        in_specs=placed,
        out_specs=(P(None, "fsdp", "tensor"), P("fsdp", "tensor", None), P("fsdp", "tensor", None)),
        check_vma=False,
    )
```

```python
import functools

import jax
import jax.numpy as jnp
from jax import lax
from jax.experimental import pallas as pl
from jax.experimental.pallas import tpu as pltpu
from jax.sharding import PartitionSpec as P

stat_decay = 0.95
graft_eps = 1e-06
Y_CHIPS = 4
TILE = 256


def kernel(
    owners,
    peers,
    code,
    block_slot,
    grads,
    stat_left,
    stat_right,
    root_left,
    root_right,
    directions,
    new_left,
    new_right,
    g_full,
    rl_full,
    pick,
    half,
    precond,
    dir_buf,
    back,
    parts,
    a2a_send,
    a2a_recv,
    back_send,
    back_recv,
    part_send,
    part_recv,
    ring_send,
    ring_recv,
):
    slots = stat_left.shape[0]
    blocks, row_share, col_share = grads.shape
    order = g_full.shape[1]
    me = lax.axis_index("fsdp")
    t = lax.axis_index("tensor")
    z_chips = owners // Y_CHIPS
    my_z, my_y = me // Y_CHIPS, me % Y_CHIPS
    x, core = t // 2, t % 2
    x_chips = peers // 2
    left = ((x + x_chips - 1) % x_chips) * 2 + core
    right = ((x + 1) % x_chips) * 2 + core
    across = ((x + 2) % x_chips) * 2 + core
    sibling = x * 2 + 1 - core

    def partner(k):
        j, dy = k // Y_CHIPS, k % Y_CHIPS
        hop = (j + 1) // 2
        dz = jnp.where(j % 2 == 1, hop, z_chips - hop)
        return ((my_z + dz) % z_chips) * Y_CHIPS + (my_y + dy) % Y_CHIPS

    def to_owner(f):
        return {"fsdp": f, "tensor": t}

    def to_peer(u):
        return {"fsdp": me, "tensor": u}

    barrier = pltpu.get_barrier_semaphore()

    def greet_owner(k, carry):
        pl.semaphore_signal(barrier, inc=1, device_id=to_owner((me + k) % owners))
        return carry

    def greet_peer(k, carry):
        pl.semaphore_signal(barrier, inc=1, device_id=to_peer((t + k) % peers))
        return carry

    lax.fori_loop(1, owners, greet_owner, 0)
    lax.fori_loop(1, peers, greet_peer, 0)
    pl.semaphore_wait(barrier, owners + peers - 2)

    def g_part(s):
        def view(u, part=None):
            cols = pl.ds(pl.multiple_of(u * col_share, col_share), col_share)
            if part is None:
                return g_full.at[s, :, cols]
            return g_full.at[s, pl.ds(part * (order // 2), order // 2), cols]

        return view

    rl_rows = root_left.shape[1]

    def rl_part(s):
        def view(u, part=None):
            if part is None:
                return rl_full.at[s, pl.ds(pl.multiple_of(u * rl_rows, rl_rows), rl_rows)]
            size = rl_rows // 2
            return rl_full.at[s, pl.ds(pl.multiple_of(u * rl_rows + part * size, size), size)]

        return view

    def push(ring, n, piece, u):
        pltpu.make_async_remote_copy(
            src_ref=piece,
            dst_ref=piece,
            send_sem=ring_send.at[ring],
            recv_sem=ring_recv.at[ring, n],
            device_id=to_peer(u),
        ).start()

    def arrive(ring, n, piece):
        pltpu.make_async_copy(piece, piece, ring_recv.at[ring, n]).wait()

    def ring_begin(ring, view):
        push(ring, 0, view(t), right)
        push(ring, 1, view(t), left)
        push(ring, 4, view(t), sibling)

    def ring_forward(ring, view):
        arrive(ring, 0, view(left))
        push(ring, 2, view(left, 0), right)
        push(ring, 5, view(left), sibling)
        arrive(ring, 1, view(right))
        push(ring, 3, view(right, 1), left)
        push(ring, 6, view(right), sibling)

    def ring_last(ring, view):
        arrive(ring, 2, view(across, 0))
        arrive(ring, 3, view(across, 1))
        push(ring, 7, view(across), sibling)

    def ring_end(ring, view):
        for n, u in ((4, t), (5, left), (6, right), (7, across)):
            arrive(ring, n, view(u // 2 * 2 + 1 - core))

    my_rows = pl.ds(pl.multiple_of(t * rl_rows, rl_rows), rl_rows)
    for s in range(slots):
        rl_full[s, my_rows, :] = root_left[s]
        ring_begin(s, rl_part(s))

    g_rows = pl.ds(pl.multiple_of(me * row_share, row_share), row_share)
    g_cols = pl.ds(pl.multiple_of(t * col_share, col_share), col_share)

    for s in range(slots):

        def give(k, carry, s=s):
            f = partner(k)
            pick[s, f] = grads[code[slots * f + s] // 2].astype(pick.dtype)
            pltpu.make_async_remote_copy(
                src_ref=pick.at[s, f],
                dst_ref=g_full.at[s, g_rows, g_cols],
                send_sem=a2a_send.at[s],
                recv_sem=a2a_recv.at[s],
                device_id=to_owner(f),
            ).start()
            return carry

        lax.fori_loop(1, owners, give, 0)
        g_full[s, g_rows, g_cols] = grads[code[slots * me + s] // 2].astype(g_full.dtype)

    def owners_but_me(ref, sem):
        whole = ref.at[pl.ds(0, owners - 1)]
        pltpu.make_async_copy(whole, whole, sem).wait()

    for s in range(slots):
        ring_forward(s, rl_part(s))

    def preconditioned(s):
        def half_tile(i, carry):
            rows = pl.ds(pl.multiple_of(i * TILE, TILE), TILE)
            half[s, rows, :] = jnp.dot(
                g_full[s, rows, :], root_right[s], preferred_element_type=jnp.float32
            ).astype(half.dtype)
            return carry

        lax.fori_loop(0, order // TILE, half_tile, 0)

        def squares(tile):
            return jnp.sum((tile * tile).reshape(-1, 8, col_share), axis=0)

        def precond_tile(i, carry):
            dir_sum, grad_sum = carry
            rows = pl.ds(pl.multiple_of(i * TILE, TILE), TILE)
            tile = jnp.dot(rl_full[s, rows, :], half[s], preferred_element_type=jnp.float32)
            precond[s, rows, :] = tile
            grad = g_full[s, rows, g_cols].astype(jnp.float32)
            return dir_sum + squares(tile), grad_sum + squares(grad)

        zero = jnp.zeros((8, col_share), jnp.float32)
        dir_sum, grad_sum = lax.fori_loop(0, order // TILE, precond_tile, (zero, zero))
        parts[s, t, 0:8] = dir_sum
        parts[s, t, 8:16] = grad_sum

        def tell(k, carry):
            pltpu.make_async_remote_copy(
                src_ref=parts.at[s, t],
                dst_ref=parts.at[s, t],
                send_sem=part_send.at[s],
                recv_sem=part_recv.at[s],
                device_id=to_peer((t + k) % peers),
            ).start()
            return carry

        lax.fori_loop(1, peers, tell, 0)

    def peers_but_me(s, sem):
        whole = parts.at[s, pl.ds(0, peers - 1)]
        pltpu.make_async_copy(whole, whole, sem).wait()

    def send_back(s):
        peers_but_me(s, part_recv.at[s])
        total = jnp.sum(parts[s], axis=0)
        dir_sq = jnp.sum(total[0:8], keepdims=True)
        grad_sq = jnp.sum(total[8:16], keepdims=True)
        scale = jnp.sqrt(grad_sq / (dir_sq + graft_eps))

        def scaled(i, carry):
            rows = pl.ds(pl.multiple_of(i * TILE, TILE), TILE)
            dir_buf[s, rows, :] = (precond[s, rows, :] * scale).astype(dir_buf.dtype)
            return carry

        lax.fori_loop(0, order // TILE, scaled, 0)

        def give(k, carry):
            f = partner(k)
            rows = pl.ds(pl.multiple_of(f * row_share, row_share), row_share)
            pltpu.make_async_remote_copy(
                src_ref=dir_buf.at[s, rows],
                dst_ref=back.at[slots * me + s],
                send_sem=back_send.at[s],
                recv_sem=back_recv.at[s],
                device_id=to_owner(f),
            ).start()
            return carry

        lax.fori_loop(1, owners, give, 0)
        back[slots * me + s] = dir_buf[s, g_rows]

    def statistics(s):
        used = code[slots * me + s] % 2 == 1

        def left_tile(i, carry):
            cols = pl.ds(pl.multiple_of(i * TILE, TILE), TILE)
            prod = lax.dot_general(
                g_full[s, my_rows, :],
                g_full[s, cols, :],
                (((1,), (1,)), ((), ())),
                preferred_element_type=jnp.float32,
            )
            old = stat_left[s, :, cols].astype(jnp.float32)
            new = jnp.where(used, stat_decay * old + (1.0 - stat_decay) * prod, old)
            new_left[s, :, cols] = new.astype(new_left.dtype)
            return carry

        def right_tile(i, carry):
            cols = pl.ds(pl.multiple_of(i * TILE, TILE), TILE)
            prod = lax.dot_general(
                g_full[s, :, g_cols],
                g_full[s, :, cols],
                (((0,), (0,)), ((), ())),
                preferred_element_type=jnp.float32,
            )
            old = stat_right[s, :, cols].astype(jnp.float32)
            new = jnp.where(used, stat_decay * old + (1.0 - stat_decay) * prod, old)
            new_right[s, :, cols] = new.astype(new_right.dtype)
            return carry

        lax.fori_loop(0, order // TILE, left_tile, 0)
        lax.fori_loop(0, order // TILE, right_tile, 0)

    owners_but_me(pick.at[0], a2a_recv.at[0])
    ring_begin(slots, g_part(0))
    for s in range(slots):
        ring_last(s, rl_part(s))
    ring_forward(slots, g_part(0))
    ring_end(0, rl_part(0))
    ring_last(slots, g_part(0))
    owners_but_me(pick.at[1], a2a_recv.at[1])
    ring_begin(slots + 1, g_part(1))
    ring_end(slots, g_part(0))
    preconditioned(0)
    ring_forward(slots + 1, g_part(1))
    send_back(0)
    ring_end(1, rl_part(1))
    ring_last(slots + 1, g_part(1))
    ring_end(slots + 1, g_part(1))
    preconditioned(1)
    send_back(1)
    statistics(0)
    statistics(1)

    for s in range(slots):
        owners_but_me(back, back_recv.at[s])

    def choose(b, carry):
        directions[b] = back[block_slot[b]]
        return carry

    lax.fori_loop(0, blocks, choose, 0)

    for s in range(slots):
        owners_but_me(pick.at[s], a2a_send.at[s])
        owners_but_me(back, back_send.at[s])
        peers_but_me(s, part_send.at[s])
        for ring in (s, slots + s):
            sent = rl_full.at[s, pl.ds(0, 7 * rl_rows)]
            pltpu.make_async_copy(sent, sent, ring_send.at[ring]).wait()


def on_device(grads, block_slot, stat_left, stat_right, root_left, root_right):
    owners = lax.axis_size("fsdp")
    peers = lax.axis_size("tensor")
    blocks, row_share, col_share = grads.shape
    slots, left_rows, order = stat_left.shape
    slot_ids = jnp.arange(owners * slots, dtype=jnp.int32)
    block_ids = jnp.arange(blocks, dtype=jnp.int32)
    match = block_slot[None, :] == slot_ids[:, None]
    code = jnp.sum(jnp.where(match, 2 * block_ids[None, :] + 1, 0), axis=1, dtype=jnp.int32)
    smem = pl.BlockSpec(memory_space=pltpu.SMEM)
    vmem = pl.BlockSpec(memory_space=pltpu.VMEM)
    bf16 = jnp.bfloat16
    dma = pltpu.SemaphoreType.DMA
    return pl.pallas_call(
        functools.partial(kernel, owners, peers),
        out_shape=(
            jax.ShapeDtypeStruct(grads.shape, bf16),
            jax.ShapeDtypeStruct(stat_left.shape, bf16),
            jax.ShapeDtypeStruct(stat_right.shape, bf16),
        ),
        in_specs=[smem, smem] + [vmem] * 5,
        out_specs=(vmem, vmem, vmem),
        scratch_shapes=[
            pltpu.VMEM((slots, order, order), bf16),
            pltpu.VMEM((slots, order, order), bf16),
            pltpu.VMEM((slots, owners, row_share, col_share), bf16),
            pltpu.VMEM((slots, order, col_share), bf16),
            pltpu.VMEM((slots, order, col_share), jnp.float32),
            pltpu.VMEM((slots, order, col_share), bf16),
            pltpu.VMEM((slots * owners, row_share, col_share), bf16),
            pltpu.VMEM((slots, peers, 16, col_share), jnp.float32),
            dma((slots,)),
            dma((slots,)),
            dma((slots,)),
            dma((slots,)),
            dma((slots,)),
            dma((slots,)),
            dma((2 * slots,)),
            dma((2 * slots, 8)),
        ],
        compiler_params=pltpu.CompilerParams(
            collective_id=0, has_side_effects=True, vmem_limit_bytes=48 * 1024 * 1024
        ),
        name="shampoo_step",
    )(code, block_slot, grads, stat_left, stat_right, root_left, root_right)


def solution(mesh):
    placed = (
        P(None, "fsdp", "tensor"),
        P(),
        P("fsdp", "tensor", None),
        P("fsdp", "tensor", None),
        P("fsdp", "tensor", None),
        P("fsdp", None, "tensor"),
    )
    return jax.shard_map(
        on_device,
        mesh=mesh,
        in_specs=placed,
        out_specs=(P(None, "fsdp", "tensor"), P("fsdp", "tensor", None), P("fsdp", "tensor", None)),
        check_vma=False,
    )
```

```python
import functools

import jax
import jax.numpy as jnp
from jax import lax
from jax.experimental import pallas as pl
from jax.experimental.pallas import tpu as pltpu
from jax.sharding import PartitionSpec as P

stat_decay = 0.95
graft_eps = 1e-06
TILE = 256
Y_CHIPS = 4


def kernel(
    owners,
    peers,
    code,
    block_slot,
    grads_hbm,
    stat_left_hbm,
    stat_right_hbm,
    root_left_hbm,
    root_right_hbm,
    directions,
    new_left_hbm,
    new_right_hbm,
    grads,
    stat_left,
    stat_right,
    root_right,
    new_left,
    new_right,
    g_full,
    rl_full,
    pick,
    half,
    dir_buf,
    back,
    parts,
    scales,
    scale_rows,
    a2a_send,
    a2a_recv,
    back_send,
    back_recv,
    part_send,
    part_recv,
    scale_send,
    scale_recv,
    ring_send,
    ring_recv,
    load_sem,
    store_sem,
):
    slots, rl_rows, _ = root_left_hbm.shape
    blocks, row_share, col_share = grads.shape
    order = g_full.shape[1]
    me = lax.axis_index("fsdp")
    t = lax.axis_index("tensor")
    z_chips = owners // Y_CHIPS
    my_z, my_y = me // Y_CHIPS, me % Y_CHIPS
    x, core = t // 2, t % 2
    x_chips = peers // 2
    left = ((x + x_chips - 1) % x_chips) * 2 + core
    right = ((x + 1) % x_chips) * 2 + core
    across = ((x + 2) % x_chips) * 2 + core
    sibling = x * 2 + 1 - core

    def partner(k):
        k = owners - k
        j, dy = k // Y_CHIPS, k % Y_CHIPS
        hop = (j + 1) // 2
        dz = jnp.where(j % 2 == 1, hop, z_chips - hop)
        return ((my_z + dz) % z_chips) * Y_CHIPS + (my_y + dy) % Y_CHIPS

    def to_owner(f):
        return {"fsdp": f, "tensor": t}

    def to_peer(u):
        return {"fsdp": me, "tensor": u}

    my_rows = pl.ds(pl.multiple_of(t * rl_rows, rl_rows), rl_rows)
    g_rows = pl.ds(pl.multiple_of(me * row_share, row_share), row_share)
    g_cols = pl.ds(pl.multiple_of(t * col_share, col_share), col_share)

    loads = [
        pltpu.make_async_copy(source, target, load_sem.at[n])
        for n, (source, target) in enumerate(
            (
                (root_left_hbm, rl_full.at[:, my_rows]),
                (grads_hbm, grads),
                (root_right_hbm, root_right),
                (stat_left_hbm, stat_left),
                (stat_right_hbm, stat_right),
            )
        )
    ]
    for load in loads:
        load.start()

    barrier = pltpu.get_barrier_semaphore()

    def greet_owner(k, carry):
        pl.semaphore_signal(barrier, inc=1, device_id=to_owner((me + k) % owners))
        return carry

    def greet_peer(k, carry):
        pl.semaphore_signal(barrier, inc=1, device_id=to_peer((t + k) % peers))
        return carry

    lax.fori_loop(1, owners, greet_owner, 0)
    lax.fori_loop(1, peers, greet_peer, 0)
    pl.semaphore_wait(barrier, owners + peers - 2)

    def g_part(s):
        def view(u, part=None):
            cols = pl.ds(pl.multiple_of(u * col_share, col_share), col_share)
            if part is None:
                return g_full.at[s, :, cols]
            return g_full.at[s, pl.ds(part * (order // 2), order // 2), cols]

        return view

    def rl_part(s):
        def view(u, part=None):
            if part is None:
                return rl_full.at[s, pl.ds(pl.multiple_of(u * rl_rows, rl_rows), rl_rows)]
            size = rl_rows // 2
            return rl_full.at[s, pl.ds(pl.multiple_of(u * rl_rows + part * size, size), size)]

        return view

    def push(ring, n, piece, u):
        pltpu.make_async_remote_copy(
            src_ref=piece,
            dst_ref=piece,
            send_sem=ring_send.at[ring],
            recv_sem=ring_recv.at[ring, n],
            device_id=to_peer(u),
        ).start()

    def arrive(ring, n, piece):
        pltpu.make_async_copy(piece, piece, ring_recv.at[ring, n]).wait()

    def ring_begin(ring, view):
        push(ring, 0, view(t, 0), right)
        push(ring, 1, view(t, 1), left)
        push(ring, 2, view(t, 1), right)
        push(ring, 3, view(t, 0), left)
        push(ring, 6, view(t), sibling)

    def ring_forward(ring, view):
        arrive(ring, 0, view(left, 0))
        push(ring, 4, view(left, 0), right)
        arrive(ring, 1, view(right, 1))
        push(ring, 5, view(right, 1), left)

    def ring_share(ring, view):
        arrive(ring, 2, view(left, 1))
        push(ring, 7, view(left), sibling)
        arrive(ring, 3, view(right, 0))
        push(ring, 8, view(right), sibling)

    def ring_last(ring, view):
        arrive(ring, 4, view(across, 0))
        arrive(ring, 5, view(across, 1))
        push(ring, 9, view(across), sibling)

    def ring_end(ring, view):
        for n, u in ((6, t), (7, left), (8, right), (9, across)):
            arrive(ring, n, view(u // 2 * 2 + 1 - core))

    def give(s):
        def one(k, carry):
            f = partner(k)
            pick[s, f] = grads[code[slots * f + s] // 2].astype(pick.dtype)
            pltpu.make_async_remote_copy(
                src_ref=pick.at[s, f],
                dst_ref=g_full.at[s, g_rows, g_cols],
                send_sem=a2a_send.at[s],
                recv_sem=a2a_recv.at[s],
                device_id=to_owner(f),
            ).start()
            return carry

        lax.fori_loop(1, owners, one, 0)
        g_full[s, g_rows, g_cols] = grads[code[slots * me + s] // 2].astype(g_full.dtype)

    def taken(ref, count, sem):
        whole = ref.at[pl.ds(0, count)]
        pltpu.make_async_copy(whole, whole, sem).wait()

    def rows_here(s):
        taken(pick.at[s], owners - 1, a2a_recv.at[s])

    def squares(tile):
        return jnp.sum((tile * tile).reshape(-1, 8, col_share), axis=0)

    def preconditioned(s):
        half[s] = jnp.dot(
            g_full[s], root_right[s], preferred_element_type=jnp.float32
        ).astype(half.dtype)
        product = jnp.dot(rl_full[s], half[s], preferred_element_type=jnp.float32)
        dir_buf[s] = product.astype(dir_buf.dtype)
        dir_sum = squares(product)

        def one(k, carry):
            f = partner(k)
            pltpu.make_async_remote_copy(
                src_ref=dir_buf.at[s, pl.ds(pl.multiple_of(f * row_share, row_share), row_share)],
                dst_ref=back.at[slots * me + s],
                send_sem=back_send.at[s],
                recv_sem=back_recv.at[s],
                device_id=to_owner(f),
            ).start()
            return carry

        lax.fori_loop(1, owners, one, 0)
        back[slots * me + s] = dir_buf[s, g_rows]
        return dir_sum

    def tell(s, dir_sum):
        parts[s, t, 0:8] = dir_sum
        parts[s, t, 8:16] = squares(g_full[s, :, g_cols].astype(jnp.float32))

        def one(k, carry):
            pltpu.make_async_remote_copy(
                src_ref=parts.at[s, t],
                dst_ref=parts.at[s, t],
                send_sem=part_send.at[s],
                recv_sem=part_recv.at[s],
                device_id=to_peer((t + k) % peers),
            ).start()
            return carry

        lax.fori_loop(1, peers, one, 0)

    def scale_of(s):
        taken(parts.at[s], peers - 1, part_recv.at[s])
        total = jnp.sum(parts[s], axis=0)
        dir_sq = jnp.sum(total[0:8], keepdims=True)
        grad_sq = jnp.sum(total[8:16], keepdims=True)
        return jnp.sqrt(grad_sq / (dir_sq + graft_eps))

    def send_scales():
        lane = lax.broadcasted_iota(jnp.int32, (1, col_share), 1)
        scales[me] = jnp.where(lane < col_share // 2, scale_of(0), scale_of(1))

        def one(k, carry):
            f = partner(k)
            pltpu.make_async_remote_copy(
                src_ref=scales.at[me],
                dst_ref=scales.at[me],
                send_sem=scale_send,
                recv_sem=scale_recv,
                device_id=to_owner(f),
            ).start()
            return carry

        lax.fori_loop(1, owners, one, 0)

    def statistics(s):
        used = code[slots * me + s] % 2 == 1

        def left_tile(i, carry):
            cols = pl.ds(pl.multiple_of(i * TILE, TILE), TILE)
            prod = lax.dot_general(
                g_full[s, my_rows, :],
                g_full[s, cols, :],
                (((1,), (1,)), ((), ())),
                preferred_element_type=jnp.float32,
            )
            old = stat_left[s, :, cols].astype(jnp.float32)
            new = jnp.where(used, stat_decay * old + (1.0 - stat_decay) * prod, old)
            new_left[s, :, cols] = new.astype(new_left.dtype)
            return carry

        def right_tile(i, carry):
            cols = pl.ds(pl.multiple_of(i * TILE, TILE), TILE)
            prod = lax.dot_general(
                g_full[s, :, g_cols],
                g_full[s, :, cols],
                (((0,), (0,)), ((), ())),
                preferred_element_type=jnp.float32,
            )
            old = stat_right[s, :, cols].astype(jnp.float32)
            new = jnp.where(used, stat_decay * old + (1.0 - stat_decay) * prod, old)
            new_right[s, :, cols] = new.astype(new_right.dtype)
            return carry

        lax.fori_loop(0, order // TILE, left_tile, 0)
        lax.fori_loop(0, order // TILE, right_tile, 0)

    g0, g1, rl0, rl1 = (slots, g_part(0)), (slots + 1, g_part(1)), (0, rl_part(0)), (1, rl_part(1))

    loads[0].wait()
    ring_begin(*rl0)
    loads[1].wait()
    give(0)
    give(1)
    ring_forward(*rl0)
    ring_begin(*rl1)
    ring_share(*rl0)
    ring_last(*rl0)
    ring_forward(*rl1)
    ring_share(*rl1)
    rows_here(0)
    ring_begin(*g0)
    ring_last(*rl1)
    ring_forward(*g0)
    ring_share(*g0)
    ring_last(*g0)
    loads[2].wait()
    ring_end(*rl0)
    ring_end(*g0)
    rows_here(1)
    ring_begin(*g1)
    dir_sum = preconditioned(0)
    tell(0, dir_sum)
    ring_forward(*g1)
    ring_share(*g1)
    ring_last(*g1)
    ring_end(*rl1)
    ring_end(*g1)
    dir_sum = preconditioned(1)
    tell(1, dir_sum)
    loads[3].wait()
    loads[4].wait()
    statistics(0)
    send_scales()
    statistics(1)
    stores = [
        pltpu.make_async_copy(new_left, new_left_hbm, store_sem.at[0]),
        pltpu.make_async_copy(new_right, new_right_hbm, store_sem.at[1]),
    ]
    for store in stores:
        store.start()

    taken(scales, owners - 1, scale_recv)
    each = scales[:, 0, :]
    for s in range(slots):
        column = each[:, s * (col_share // 2) : s * (col_share // 2) + 1]
        scale_rows[s * owners : (s + 1) * owners, :] = jnp.broadcast_to(column, (owners, col_share))
    for s in range(slots):
        taken(back, owners - 1, back_recv.at[s])

    def choose(b, carry):
        slot = block_slot[b]
        scale = scale_rows[pl.ds(slot % slots * owners + slot // slots, 1), :]
        directions[b] = (back[slot].astype(jnp.float32) * scale).astype(directions.dtype)
        return carry

    lax.fori_loop(0, blocks, choose, 0)

    for store in stores:
        store.wait()
    taken(scales, owners - 1, scale_send)
    for s in range(slots):
        taken(pick.at[s], owners - 1, a2a_send.at[s])
        taken(back, owners - 1, back_send.at[s])
        taken(parts.at[s], peers - 1, part_send.at[s])
        for ring in (s, slots + s):
            sent = rl_full.at[s, pl.ds(0, 7 * rl_rows)]
            pltpu.make_async_copy(sent, sent, ring_send.at[ring]).wait()


def on_device(grads, block_slot, stat_left, stat_right, root_left, root_right):
    owners = lax.axis_size("fsdp")
    peers = lax.axis_size("tensor")
    blocks, row_share, col_share = grads.shape
    slots, left_rows, order = stat_left.shape
    slot_ids = jnp.arange(owners * slots, dtype=jnp.int32)
    block_ids = jnp.arange(blocks, dtype=jnp.int32)
    match = block_slot[None, :] == slot_ids[:, None]
    code = jnp.sum(jnp.where(match, 2 * block_ids[None, :] + 1, 0), axis=1, dtype=jnp.int32)
    smem = pl.BlockSpec(memory_space=pltpu.SMEM)
    vmem = pl.BlockSpec(memory_space=pltpu.VMEM)
    hbm = pl.BlockSpec(memory_space=pltpu.HBM)
    bf16 = jnp.bfloat16
    dma = pltpu.SemaphoreType.DMA
    return pl.pallas_call(
        functools.partial(kernel, owners, peers),
        out_shape=(
            jax.ShapeDtypeStruct(grads.shape, bf16),
            jax.ShapeDtypeStruct(stat_left.shape, bf16),
            jax.ShapeDtypeStruct(stat_right.shape, bf16),
        ),
        in_specs=[smem, smem] + [hbm] * 5,
        out_specs=(vmem, hbm, hbm),
        scratch_shapes=[
            pltpu.VMEM(grads.shape, grads.dtype),
            pltpu.VMEM(stat_left.shape, bf16),
            pltpu.VMEM(stat_right.shape, bf16),
            pltpu.VMEM(root_right.shape, bf16),
            pltpu.VMEM(stat_left.shape, bf16),
            pltpu.VMEM(stat_right.shape, bf16),
            pltpu.VMEM((slots, order, order), bf16),
            pltpu.VMEM((slots, order, order), bf16),
            pltpu.VMEM((slots, owners, row_share, col_share), bf16),
            pltpu.VMEM((slots, order, col_share), bf16),
            pltpu.VMEM((slots, order, col_share), bf16),
            pltpu.VMEM((slots * owners, row_share, col_share), bf16),
            pltpu.VMEM((slots, peers, 16, col_share), jnp.float32),
            pltpu.VMEM((owners, 1, col_share), jnp.float32),
            pltpu.VMEM((slots * owners, col_share), jnp.float32),
            dma((slots,)),
            dma((slots,)),
            dma((slots,)),
            dma((slots,)),
            dma((slots,)),
            dma((slots,)),
            dma(()),
            dma(()),
            dma((2 * slots,)),
            dma((2 * slots, 10)),
            dma((5,)),
            dma((2,)),
        ],
        compiler_params=pltpu.CompilerParams(
            collective_id=0, has_side_effects=True, vmem_limit_bytes=52 * 1024 * 1024
        ),
        name="shampoo_step",
    )(code, block_slot, grads, stat_left, stat_right, root_left, root_right)


def solution(mesh):
    placed = (
        P(None, "fsdp", "tensor"),
        P(),
        P("fsdp", "tensor", None),
        P("fsdp", "tensor", None),
        P("fsdp", "tensor", None),
        P("fsdp", None, "tensor"),
    )
    return jax.shard_map(
        on_device,
        mesh=mesh,
        in_specs=placed,
        out_specs=(P(None, "fsdp", "tensor"), P("fsdp", "tensor", None), P("fsdp", "tensor", None)),
        check_vma=False,
    )
```

```python
import functools

import jax
import jax.numpy as jnp
from jax import lax
from jax.experimental import pallas as pl
from jax.experimental.pallas import tpu as pltpu
from jax.sharding import PartitionSpec as P

stat_decay = 0.95
graft_eps = 1e-06
TILE = 256
Y_CHIPS = 4


def kernel(
    owners,
    peers,
    code,
    block_slot,
    grads_hbm,
    stat_left_hbm,
    stat_right_hbm,
    root_left_hbm,
    root_right_hbm,
    directions,
    new_left_hbm,
    new_right_hbm,
    grads,
    stat_left,
    stat_right,
    root_right,
    new_left,
    new_right,
    g_full,
    rl_full,
    pick,
    half,
    half_sum,
    dir_buf,
    back,
    parts,
    scales,
    scale_rows,
    a2a_send,
    a2a_recv,
    back_send,
    back_recv,
    part_send,
    part_recv,
    scale_send,
    scale_recv,
    ring_send,
    ring_recv,
    load_sem,
    store_sem,
):
    slots, rl_rows, _ = root_left_hbm.shape
    blocks, row_share, col_share = grads.shape
    order = g_full.shape[1]
    me = lax.axis_index("fsdp")
    t = lax.axis_index("tensor")
    z_chips = owners // Y_CHIPS
    my_z, my_y = me // Y_CHIPS, me % Y_CHIPS
    x, core = t // 2, t % 2
    x_chips = peers // 2
    left = ((x + x_chips - 1) % x_chips) * 2 + core
    right = ((x + 1) % x_chips) * 2 + core
    across = ((x + 2) % x_chips) * 2 + core
    sibling = x * 2 + 1 - core

    def partner(k):
        k = owners - k
        j, dy = k // Y_CHIPS, k % Y_CHIPS
        hop = (j + 1) // 2
        dz = jnp.where(j % 2 == 1, hop, z_chips - hop)
        return ((my_z + dz) % z_chips) * Y_CHIPS + (my_y + dy) % Y_CHIPS

    def to_owner(f):
        return {"fsdp": f, "tensor": t}

    def to_peer(u):
        return {"fsdp": me, "tensor": u}

    my_rows = pl.ds(pl.multiple_of(t * rl_rows, rl_rows), rl_rows)
    g_rows = pl.ds(pl.multiple_of(me * row_share, row_share), row_share)
    g_cols = pl.ds(pl.multiple_of(t * col_share, col_share), col_share)

    loads = [
        pltpu.make_async_copy(source, target, load_sem.at[n])
        for n, (source, target) in enumerate(
            (
                (root_left_hbm, rl_full.at[:, my_rows]),
                (grads_hbm, grads),
                (root_right_hbm, root_right),
                (stat_left_hbm, stat_left),
                (stat_right_hbm, stat_right),
            )
        )
    ]
    for load in loads:
        load.start()

    barrier = pltpu.get_barrier_semaphore()

    def greet_owner(k, carry):
        pl.semaphore_signal(barrier, inc=1, device_id=to_owner((me + k) % owners))
        return carry

    def greet_peer(k, carry):
        pl.semaphore_signal(barrier, inc=1, device_id=to_peer((t + k) % peers))
        return carry

    lax.fori_loop(1, owners, greet_owner, 0)
    lax.fori_loop(1, peers, greet_peer, 0)
    pl.semaphore_wait(barrier, owners + peers - 2)

    def g_part(s):
        def view(u, part=None):
            cols = pl.ds(pl.multiple_of(u * col_share, col_share), col_share)
            if part is None:
                return g_full.at[s, :, cols]
            return g_full.at[s, pl.ds(part * (order // 2), order // 2), cols]

        return view

    def rl_part(s):
        def view(u, part=None):
            if part is None:
                return rl_full.at[s, pl.ds(pl.multiple_of(u * rl_rows, rl_rows), rl_rows)]
            size = rl_rows // 2
            return rl_full.at[s, pl.ds(pl.multiple_of(u * rl_rows + part * size, size), size)]

        return view

    def push(ring, n, piece, u):
        pltpu.make_async_remote_copy(
            src_ref=piece,
            dst_ref=piece,
            send_sem=ring_send.at[ring],
            recv_sem=ring_recv.at[ring, n],
            device_id=to_peer(u),
        ).start()

    def arrive(ring, n, piece):
        pltpu.make_async_copy(piece, piece, ring_recv.at[ring, n]).wait()

    def ring_begin(ring, view):
        push(ring, 0, view(t, 0), right)
        push(ring, 1, view(t, 1), left)
        push(ring, 2, view(t, 1), right)
        push(ring, 3, view(t, 0), left)
        push(ring, 6, view(t), sibling)

    def ring_forward(ring, view):
        arrive(ring, 0, view(left, 0))
        push(ring, 4, view(left, 0), right)
        arrive(ring, 1, view(right, 1))
        push(ring, 5, view(right, 1), left)

    def ring_share(ring, view):
        arrive(ring, 2, view(left, 1))
        push(ring, 7, view(left), sibling)
        arrive(ring, 3, view(right, 0))
        push(ring, 8, view(right), sibling)

    def ring_last(ring, view):
        arrive(ring, 4, view(across, 0))
        arrive(ring, 5, view(across, 1))
        push(ring, 9, view(across), sibling)

    def ring_end(ring, view):
        for n, u in ((6, t), (7, left), (8, right), (9, across)):
            arrive(ring, n, view(u // 2 * 2 + 1 - core))

    def give(s):
        def one(k, carry):
            f = partner(k)
            pick[s, f] = grads[code[slots * f + s] // 2].astype(pick.dtype)
            pltpu.make_async_remote_copy(
                src_ref=pick.at[s, f],
                dst_ref=g_full.at[s, g_rows, g_cols],
                send_sem=a2a_send.at[s],
                recv_sem=a2a_recv.at[s],
                device_id=to_owner(f),
            ).start()
            return carry

        lax.fori_loop(1, owners, one, 0)
        g_full[s, g_rows, g_cols] = grads[code[slots * me + s] // 2].astype(g_full.dtype)

    def taken(ref, count, sem):
        whole = ref.at[pl.ds(0, count)]
        pltpu.make_async_copy(whole, whole, sem).wait()

    def rows_here(s):
        taken(pick.at[s], owners - 1, a2a_recv.at[s])

    def squares(tile):
        return jnp.sum((tile * tile).reshape(-1, 8, col_share), axis=0)

    def half_whole(s):
        half[s] = jnp.dot(
            g_full[s], root_right[s], preferred_element_type=jnp.float32
        ).astype(half.dtype)

    def half_part(s, u):
        cols = pl.ds(pl.multiple_of(u // 2 * 2 * col_share, 2 * col_share), 2 * col_share)
        return jnp.dot(
            g_full[s, :, cols], root_right[s, cols, :], preferred_element_type=jnp.float32
        )

    def half_late(s, ring, view):
        for n, u in ((6, t), (7, left), (8, right)):
            arrive(ring, n, view(u // 2 * 2 + 1 - core))
        half_sum[...] = half_part(s, t) + half_part(s, left) + half_part(s, right)
        arrive(ring, 9, view(across // 2 * 2 + 1 - core))
        half[s] = (half_sum[...] + half_part(s, across)).astype(half.dtype)

    def preconditioned(s):
        product = jnp.dot(rl_full[s], half[s], preferred_element_type=jnp.float32)
        dir_buf[s] = product.astype(dir_buf.dtype)
        dir_sum = squares(product)

        def one(k, carry):
            f = partner(k)
            pltpu.make_async_remote_copy(
                src_ref=dir_buf.at[s, pl.ds(pl.multiple_of(f * row_share, row_share), row_share)],
                dst_ref=back.at[slots * me + s],
                send_sem=back_send.at[s],
                recv_sem=back_recv.at[s],
                device_id=to_owner(f),
            ).start()
            return carry

        lax.fori_loop(1, owners, one, 0)
        back[slots * me + s] = dir_buf[s, g_rows]
        return dir_sum

    def tell(s, dir_sum):
        parts[s, t, 0:8] = dir_sum
        parts[s, t, 8:16] = squares(g_full[s, :, g_cols].astype(jnp.float32))

        def one(k, carry):
            pltpu.make_async_remote_copy(
                src_ref=parts.at[s, t],
                dst_ref=parts.at[s, t],
                send_sem=part_send.at[s],
                recv_sem=part_recv.at[s],
                device_id=to_peer((t + k) % peers),
            ).start()
            return carry

        lax.fori_loop(1, peers, one, 0)

    def scale_of(s):
        taken(parts.at[s], peers - 1, part_recv.at[s])
        total = jnp.sum(parts[s], axis=0)
        dir_sq = jnp.sum(total[0:8], keepdims=True)
        grad_sq = jnp.sum(total[8:16], keepdims=True)
        return jnp.sqrt(grad_sq / (dir_sq + graft_eps))

    def send_scales():
        lane = lax.broadcasted_iota(jnp.int32, (1, col_share), 1)
        scales[me] = jnp.where(lane < col_share // 2, scale_of(0), scale_of(1))

        def one(k, carry):
            f = partner(k)
            pltpu.make_async_remote_copy(
                src_ref=scales.at[me],
                dst_ref=scales.at[me],
                send_sem=scale_send,
                recv_sem=scale_recv,
                device_id=to_owner(f),
            ).start()
            return carry

        lax.fori_loop(1, owners, one, 0)

    def statistics(s):
        used = code[slots * me + s] % 2 == 1

        def left_tile(i, carry):
            cols = pl.ds(pl.multiple_of(i * TILE, TILE), TILE)
            prod = lax.dot_general(
                g_full[s, my_rows, :],
                g_full[s, cols, :],
                (((1,), (1,)), ((), ())),
                preferred_element_type=jnp.float32,
            )
            old = stat_left[s, :, cols].astype(jnp.float32)
            new = jnp.where(used, stat_decay * old + (1.0 - stat_decay) * prod, old)
            new_left[s, :, cols] = new.astype(new_left.dtype)
            return carry

        def right_tile(i, carry):
            cols = pl.ds(pl.multiple_of(i * TILE, TILE), TILE)
            prod = lax.dot_general(
                g_full[s, :, g_cols],
                g_full[s, :, cols],
                (((0,), (0,)), ((), ())),
                preferred_element_type=jnp.float32,
            )
            old = stat_right[s, :, cols].astype(jnp.float32)
            new = jnp.where(used, stat_decay * old + (1.0 - stat_decay) * prod, old)
            new_right[s, :, cols] = new.astype(new_right.dtype)
            return carry

        lax.fori_loop(0, order // TILE, left_tile, 0)
        lax.fori_loop(0, order // TILE, right_tile, 0)

    g0, g1, rl0, rl1 = (slots, g_part(0)), (slots + 1, g_part(1)), (0, rl_part(0)), (1, rl_part(1))

    loads[0].wait()
    ring_begin(*rl0)
    loads[1].wait()
    give(0)
    give(1)
    ring_forward(*rl0)
    ring_begin(*rl1)
    ring_share(*rl0)
    ring_last(*rl0)
    ring_forward(*rl1)
    rows_here(0)
    ring_begin(*g0)
    ring_share(*rl1)
    ring_last(*rl1)
    ring_forward(*g0)
    ring_share(*g0)
    rows_here(1)
    ring_begin(*g1)
    ring_last(*g0)
    loads[2].wait()
    ring_end(*rl0)
    ring_end(*g0)
    half_whole(0)
    dir_sum = preconditioned(0)
    tell(0, dir_sum)
    ring_forward(*g1)
    ring_share(*g1)
    ring_last(*g1)
    ring_end(*rl1)
    half_late(1, *g1)
    dir_sum = preconditioned(1)
    tell(1, dir_sum)
    loads[3].wait()
    loads[4].wait()
    statistics(0)
    send_scales()
    statistics(1)
    stores = [
        pltpu.make_async_copy(new_left, new_left_hbm, store_sem.at[0]),
        pltpu.make_async_copy(new_right, new_right_hbm, store_sem.at[1]),
    ]
    for store in stores:
        store.start()

    taken(scales, owners - 1, scale_recv)
    each = scales[:, 0, :]
    for s in range(slots):
        column = each[:, s * (col_share // 2) : s * (col_share // 2) + 1]
        scale_rows[s * owners : (s + 1) * owners, :] = jnp.broadcast_to(column, (owners, col_share))
    for s in range(slots):
        taken(back, owners - 1, back_recv.at[s])

    def choose(b, carry):
        slot = block_slot[b]
        scale = scale_rows[pl.ds(slot % slots * owners + slot // slots, 1), :]
        directions[b] = (back[slot].astype(jnp.float32) * scale).astype(directions.dtype)
        return carry

    lax.fori_loop(0, blocks, choose, 0, unroll=8)

    for store in stores:
        store.wait()
    taken(scales, owners - 1, scale_send)
    for s in range(slots):
        taken(pick.at[s], owners - 1, a2a_send.at[s])
        taken(back, owners - 1, back_send.at[s])
        taken(parts.at[s], peers - 1, part_send.at[s])
        for ring in (s, slots + s):
            sent = rl_full.at[s, pl.ds(0, 7 * rl_rows)]
            pltpu.make_async_copy(sent, sent, ring_send.at[ring]).wait()


def on_device(grads, block_slot, stat_left, stat_right, root_left, root_right):
    owners = lax.axis_size("fsdp")
    peers = lax.axis_size("tensor")
    blocks, row_share, col_share = grads.shape
    slots, left_rows, order = stat_left.shape
    slot_ids = jnp.arange(owners * slots, dtype=jnp.int32)
    block_ids = jnp.arange(blocks, dtype=jnp.int32)
    match = block_slot[None, :] == slot_ids[:, None]
    code = jnp.sum(jnp.where(match, 2 * block_ids[None, :] + 1, 0), axis=1, dtype=jnp.int32)
    smem = pl.BlockSpec(memory_space=pltpu.SMEM)
    vmem = pl.BlockSpec(memory_space=pltpu.VMEM)
    hbm = pl.BlockSpec(memory_space=pltpu.HBM)
    bf16 = jnp.bfloat16
    dma = pltpu.SemaphoreType.DMA
    return pl.pallas_call(
        functools.partial(kernel, owners, peers),
        out_shape=(
            jax.ShapeDtypeStruct(grads.shape, bf16),
            jax.ShapeDtypeStruct(stat_left.shape, bf16),
            jax.ShapeDtypeStruct(stat_right.shape, bf16),
        ),
        in_specs=[smem, smem] + [hbm] * 5,
        out_specs=(vmem, hbm, hbm),
        scratch_shapes=[
            pltpu.VMEM(grads.shape, grads.dtype),
            pltpu.VMEM(stat_left.shape, bf16),
            pltpu.VMEM(stat_right.shape, bf16),
            pltpu.VMEM(root_right.shape, bf16),
            pltpu.VMEM(stat_left.shape, bf16),
            pltpu.VMEM(stat_right.shape, bf16),
            pltpu.VMEM((slots, order, order), bf16),
            pltpu.VMEM((slots, order, order), bf16),
            pltpu.VMEM((slots, owners, row_share, col_share), bf16),
            pltpu.VMEM((slots, order, col_share), bf16),
            pltpu.VMEM((order, col_share), jnp.float32),
            pltpu.VMEM((slots, order, col_share), bf16),
            pltpu.VMEM((slots * owners, row_share, col_share), bf16),
            pltpu.VMEM((slots, peers, 16, col_share), jnp.float32),
            pltpu.VMEM((owners, 1, col_share), jnp.float32),
            pltpu.VMEM((slots * owners, col_share), jnp.float32),
            dma((slots,)),
            dma((slots,)),
            dma((slots,)),
            dma((slots,)),
            dma((slots,)),
            dma((slots,)),
            dma(()),
            dma(()),
            dma((2 * slots,)),
            dma((2 * slots, 10)),
            dma((5,)),
            dma((2,)),
        ],
        compiler_params=pltpu.CompilerParams(
            collective_id=0, has_side_effects=True, vmem_limit_bytes=105 * 512 * 1024
        ),
        name="shampoo_step",
    )(code, block_slot, grads, stat_left, stat_right, root_left, root_right)


def solution(mesh):
    placed = (
        P(None, "fsdp", "tensor"),
        P(),
        P("fsdp", "tensor", None),
        P("fsdp", "tensor", None),
        P("fsdp", "tensor", None),
        P("fsdp", None, "tensor"),
    )
    return jax.shard_map(
        on_device,
        mesh=mesh,
        in_specs=placed,
        out_specs=(P(None, "fsdp", "tensor"), P("fsdp", "tensor", None), P("fsdp", "tensor", None)),
        check_vma=False,
    )
```

```python
import functools

import jax
import jax.numpy as jnp
from jax import lax
from jax.experimental import pallas as pl
from jax.experimental.pallas import tpu as pltpu
from jax.sharding import PartitionSpec as P

stat_decay = 0.95
graft_eps = 1e-06
TILE = 256
Y_CHIPS = 4


def kernel(
    owners,
    peers,
    code,
    block_slot,
    grads_hbm,
    stat_left_hbm,
    stat_right_hbm,
    root_left_hbm,
    root_right_hbm,
    directions,
    new_left_hbm,
    new_right_hbm,
    grads,
    stat_left,
    stat_right,
    root_right,
    new_left,
    new_right,
    g_full,
    rl_full,
    pick,
    half,
    half_sum,
    dir_buf,
    back,
    parts,
    scales,
    scale_rows,
    a2a_send,
    a2a_recv,
    back_send,
    back_recv,
    part_send,
    part_recv,
    scale_send,
    scale_recv,
    ring_send,
    ring_recv,
    load_sem,
    store_sem,
):
    slots, rl_rows, _ = root_left_hbm.shape
    blocks, row_share, col_share = grads.shape
    order = g_full.shape[1]
    me = lax.axis_index("fsdp")
    t = lax.axis_index("tensor")
    z_chips = owners // Y_CHIPS
    my_z, my_y = me // Y_CHIPS, me % Y_CHIPS
    x, core = t // 2, t % 2
    x_chips = peers // 2
    left = ((x + x_chips - 1) % x_chips) * 2 + core
    right = ((x + 1) % x_chips) * 2 + core
    across = ((x + 2) % x_chips) * 2 + core
    sibling = x * 2 + 1 - core

    def partner(k):
        k = owners - k
        j, dy = k // Y_CHIPS, k % Y_CHIPS
        hop = (j + 1) // 2
        dz = jnp.where(j % 2 == 1, hop, z_chips - hop)
        return ((my_z + dz) % z_chips) * Y_CHIPS + (my_y + dy) % Y_CHIPS

    def to_owner(f):
        return {"fsdp": f, "tensor": t}

    def to_peer(u):
        return {"fsdp": me, "tensor": u}

    my_rows = pl.ds(pl.multiple_of(t * rl_rows, rl_rows), rl_rows)
    g_rows = pl.ds(pl.multiple_of(me * row_share, row_share), row_share)
    g_cols = pl.ds(pl.multiple_of(t * col_share, col_share), col_share)

    loads = [
        pltpu.make_async_copy(source, target, load_sem.at[n])
        for n, (source, target) in enumerate(
            (
                (root_left_hbm, rl_full.at[:, my_rows]),
                (grads_hbm, grads),
                (root_right_hbm, root_right),
                (stat_left_hbm, stat_left),
                (stat_right_hbm, stat_right),
            )
        )
    ]
    for load in loads:
        load.start()

    barrier = pltpu.get_barrier_semaphore()

    def greet_owner(k, carry):
        pl.semaphore_signal(barrier, inc=1, device_id=to_owner((me + k) % owners))
        return carry

    def greet_peer(k, carry):
        pl.semaphore_signal(barrier, inc=1, device_id=to_peer((t + k) % peers))
        return carry

    lax.fori_loop(1, owners, greet_owner, 0, unroll=9)
    lax.fori_loop(1, peers, greet_peer, 0)
    pl.semaphore_wait(barrier, owners + peers - 2)

    def g_part(s):
        def view(u, part=None):
            cols = pl.ds(pl.multiple_of(u * col_share, col_share), col_share)
            if part is None:
                return g_full.at[s, :, cols]
            return g_full.at[s, pl.ds(part * (order // 2), order // 2), cols]

        return view

    def rl_part(s):
        def view(u, part=None):
            if part is None:
                return rl_full.at[s, pl.ds(pl.multiple_of(u * rl_rows, rl_rows), rl_rows)]
            size = rl_rows // 2
            return rl_full.at[s, pl.ds(pl.multiple_of(u * rl_rows + part * size, size), size)]

        return view

    def push(ring, n, piece, u):
        pltpu.make_async_remote_copy(
            src_ref=piece,
            dst_ref=piece,
            send_sem=ring_send.at[ring],
            recv_sem=ring_recv.at[ring, n],
            device_id=to_peer(u),
        ).start()

    def arrive(ring, n, piece):
        pltpu.make_async_copy(piece, piece, ring_recv.at[ring, n]).wait()

    def ring_begin(ring, view):
        push(ring, 0, view(t, 0), right)
        push(ring, 1, view(t, 1), left)
        push(ring, 2, view(t, 1), right)
        push(ring, 3, view(t, 0), left)
        push(ring, 6, view(t), sibling)

    def ring_forward(ring, view):
        arrive(ring, 0, view(left, 0))
        push(ring, 4, view(left, 0), right)
        arrive(ring, 1, view(right, 1))
        push(ring, 5, view(right, 1), left)

    def ring_share(ring, view):
        arrive(ring, 2, view(left, 1))
        push(ring, 7, view(left), sibling)
        arrive(ring, 3, view(right, 0))
        push(ring, 8, view(right), sibling)

    def ring_last(ring, view):
        arrive(ring, 4, view(across, 0))
        push(ring, 9, view(across, 0), sibling)
        arrive(ring, 5, view(across, 1))
        push(ring, 10, view(across, 1), sibling)

    def across_end(ring, view):
        for part in range(2):
            arrive(ring, 9 + part, view(across // 2 * 2 + 1 - core, part))

    def ring_end(ring, view):
        for n, u in ((6, t), (7, left), (8, right)):
            arrive(ring, n, view(u // 2 * 2 + 1 - core))
        across_end(ring, view)

    def give(s):
        def one(k, carry):
            f = partner(k)
            pick[s, f] = grads[code[slots * f + s] // 2].astype(pick.dtype)
            pltpu.make_async_remote_copy(
                src_ref=pick.at[s, f],
                dst_ref=g_full.at[s, g_rows, g_cols],
                send_sem=a2a_send.at[s],
                recv_sem=a2a_recv.at[s],
                device_id=to_owner(f),
            ).start()
            return carry

        lax.fori_loop(1, owners, one, 0)
        g_full[s, g_rows, g_cols] = grads[code[slots * me + s] // 2].astype(g_full.dtype)

    def taken(ref, count, sem):
        whole = ref.at[pl.ds(0, count)]
        pltpu.make_async_copy(whole, whole, sem).wait()

    def rows_here(s):
        taken(pick.at[s], owners - 1, a2a_recv.at[s])

    def squares(tile):
        return jnp.sum((tile * tile).reshape(-1, 8, col_share), axis=0)

    def half_whole(s):
        half[s] = jnp.dot(
            g_full[s], root_right[s], preferred_element_type=jnp.float32
        ).astype(half.dtype)

    def half_part(s, u):
        cols = pl.ds(pl.multiple_of(u // 2 * 2 * col_share, 2 * col_share), 2 * col_share)
        return jnp.dot(
            g_full[s, :, cols], root_right[s, cols, :], preferred_element_type=jnp.float32
        )

    def half_late(s, ring, view):
        for n, u in ((6, t), (7, left), (8, right)):
            arrive(ring, n, view(u // 2 * 2 + 1 - core))
        half_sum[...] = half_part(s, t) + half_part(s, left) + half_part(s, right)
        across_end(ring, view)
        half[s] = (half_sum[...] + half_part(s, across)).astype(half.dtype)

    def preconditioned(s):
        product = jnp.dot(rl_full[s], half[s], preferred_element_type=jnp.float32)
        dir_buf[s] = product.astype(dir_buf.dtype)
        dir_sum = squares(product)

        def one(k, carry):
            f = partner(k)
            pltpu.make_async_remote_copy(
                src_ref=dir_buf.at[s, pl.ds(pl.multiple_of(f * row_share, row_share), row_share)],
                dst_ref=back.at[slots * me + s],
                send_sem=back_send.at[s],
                recv_sem=back_recv.at[s],
                device_id=to_owner(f),
            ).start()
            return carry

        lax.fori_loop(1, owners, one, 0)
        back[slots * me + s] = dir_buf[s, g_rows]
        return dir_sum

    def tell(s, dir_sum):
        parts[s, t, 0:8] = dir_sum
        parts[s, t, 8:16] = squares(g_full[s, :, g_cols].astype(jnp.float32))

        def one(k, carry):
            pltpu.make_async_remote_copy(
                src_ref=parts.at[s, t],
                dst_ref=parts.at[s, t],
                send_sem=part_send.at[s],
                recv_sem=part_recv.at[s],
                device_id=to_peer((t + k) % peers),
            ).start()
            return carry

        lax.fori_loop(1, peers, one, 0)

    def scale_of(s):
        taken(parts.at[s], peers - 1, part_recv.at[s])
        total = jnp.sum(parts[s], axis=0)
        dir_sq = jnp.sum(total[0:8], keepdims=True)
        grad_sq = jnp.sum(total[8:16], keepdims=True)
        return jnp.sqrt(grad_sq / (dir_sq + graft_eps))

    def send_scales():
        lane = lax.broadcasted_iota(jnp.int32, (1, col_share), 1)
        scales[me] = jnp.where(lane < col_share // 2, scale_of(0), scale_of(1))

        def one(k, carry):
            f = partner(k)
            pltpu.make_async_remote_copy(
                src_ref=scales.at[me],
                dst_ref=scales.at[me],
                send_sem=scale_send,
                recv_sem=scale_recv,
                device_id=to_owner(f),
            ).start()
            return carry

        lax.fori_loop(1, owners, one, 0)

    def statistics(s):
        used = code[slots * me + s] % 2 == 1

        def left_tile(i, carry):
            cols = pl.ds(pl.multiple_of(i * TILE, TILE), TILE)
            prod = lax.dot_general(
                g_full[s, my_rows, :],
                g_full[s, cols, :],
                (((1,), (1,)), ((), ())),
                preferred_element_type=jnp.float32,
            )
            old = stat_left[s, :, cols].astype(jnp.float32)
            new = jnp.where(used, stat_decay * old + (1.0 - stat_decay) * prod, old)
            new_left[s, :, cols] = new.astype(new_left.dtype)
            return carry

        def right_tile(i, carry):
            cols = pl.ds(pl.multiple_of(i * TILE, TILE), TILE)
            prod = lax.dot_general(
                g_full[s, :, g_cols],
                g_full[s, :, cols],
                (((0,), (0,)), ((), ())),
                preferred_element_type=jnp.float32,
            )
            old = stat_right[s, :, cols].astype(jnp.float32)
            new = jnp.where(used, stat_decay * old + (1.0 - stat_decay) * prod, old)
            new_right[s, :, cols] = new.astype(new_right.dtype)
            return carry

        lax.fori_loop(0, order // TILE, left_tile, 0)
        lax.fori_loop(0, order // TILE, right_tile, 0)

    g0, g1, rl0, rl1 = (slots, g_part(0)), (slots + 1, g_part(1)), (0, rl_part(0)), (1, rl_part(1))

    loads[0].wait()
    ring_begin(*rl0)
    loads[1].wait()
    give(0)
    give(1)
    ring_forward(*rl0)
    ring_begin(*rl1)
    ring_share(*rl0)
    ring_last(*rl0)
    ring_forward(*rl1)
    rows_here(0)
    ring_begin(*g0)
    ring_share(*rl1)
    ring_last(*rl1)
    ring_forward(*g0)
    ring_share(*g0)
    rows_here(1)
    ring_begin(*g1)
    ring_last(*g0)
    loads[2].wait()
    ring_end(*rl0)
    ring_end(*g0)
    half_whole(0)
    dir_sum = preconditioned(0)
    tell(0, dir_sum)
    ring_forward(*g1)
    ring_share(*g1)
    ring_last(*g1)
    ring_end(*rl1)
    half_late(1, *g1)
    dir_sum = preconditioned(1)
    tell(1, dir_sum)
    loads[3].wait()
    loads[4].wait()
    statistics(0)
    send_scales()
    statistics(1)
    stores = [
        pltpu.make_async_copy(new_left, new_left_hbm, store_sem.at[0]),
        pltpu.make_async_copy(new_right, new_right_hbm, store_sem.at[1]),
    ]
    for store in stores:
        store.start()

    taken(scales, owners - 1, scale_recv)
    each = scales[:, 0, :]
    for s in range(slots):
        column = each[:, s * (col_share // 2) : s * (col_share // 2) + 1]
        scale_rows[s * owners : (s + 1) * owners, :] = jnp.broadcast_to(column, (owners, col_share))
    for s in range(slots):
        taken(back, owners - 1, back_recv.at[s])

    def choose(b, carry):
        slot = block_slot[b]
        scale = scale_rows[pl.ds(slot % slots * owners + slot // slots, 1), :]
        directions[b] = (back[slot].astype(jnp.float32) * scale).astype(directions.dtype)
        return carry

    lax.fori_loop(0, blocks, choose, 0, unroll=8)

    for store in stores:
        store.wait()
    taken(scales, owners - 1, scale_send)
    for s in range(slots):
        taken(pick.at[s], owners - 1, a2a_send.at[s])
        taken(back, owners - 1, back_send.at[s])
        taken(parts.at[s], peers - 1, part_send.at[s])
        for ring in (s, slots + s):
            sent = rl_full.at[s, pl.ds(0, 7 * rl_rows)]
            pltpu.make_async_copy(sent, sent, ring_send.at[ring]).wait()


def on_device(grads, block_slot, stat_left, stat_right, root_left, root_right):
    owners = lax.axis_size("fsdp")
    peers = lax.axis_size("tensor")
    blocks, row_share, col_share = grads.shape
    slots, left_rows, order = stat_left.shape
    slot_ids = jnp.arange(owners * slots, dtype=jnp.int32)
    block_ids = jnp.arange(blocks, dtype=jnp.int32)
    match = block_slot[None, :] == slot_ids[:, None]
    code = jnp.sum(jnp.where(match, 2 * block_ids[None, :] + 1, 0), axis=1, dtype=jnp.int32)
    smem = pl.BlockSpec(memory_space=pltpu.SMEM)
    vmem = pl.BlockSpec(memory_space=pltpu.VMEM)
    hbm = pl.BlockSpec(memory_space=pltpu.HBM)
    bf16 = jnp.bfloat16
    dma = pltpu.SemaphoreType.DMA
    return pl.pallas_call(
        functools.partial(kernel, owners, peers),
        out_shape=(
            jax.ShapeDtypeStruct(grads.shape, bf16),
            jax.ShapeDtypeStruct(stat_left.shape, bf16),
            jax.ShapeDtypeStruct(stat_right.shape, bf16),
        ),
        in_specs=[smem, smem] + [hbm] * 5,
        out_specs=(vmem, hbm, hbm),
        scratch_shapes=[
            pltpu.VMEM(grads.shape, grads.dtype),
            pltpu.VMEM(stat_left.shape, bf16),
            pltpu.VMEM(stat_right.shape, bf16),
            pltpu.VMEM(root_right.shape, bf16),
            pltpu.VMEM(stat_left.shape, bf16),
            pltpu.VMEM(stat_right.shape, bf16),
            pltpu.VMEM((slots, order, order), bf16),
            pltpu.VMEM((slots, order, order), bf16),
            pltpu.VMEM((slots, owners, row_share, col_share), bf16),
            pltpu.VMEM((slots, order, col_share), bf16),
            pltpu.VMEM((order, col_share), jnp.float32),
            pltpu.VMEM((slots, order, col_share), bf16),
            pltpu.VMEM((slots * owners, row_share, col_share), bf16),
            pltpu.VMEM((slots, peers, 16, col_share), jnp.float32),
            pltpu.VMEM((owners, 1, col_share), jnp.float32),
            pltpu.VMEM((slots * owners, col_share), jnp.float32),
            dma((slots,)),
            dma((slots,)),
            dma((slots,)),
            dma((slots,)),
            dma((slots,)),
            dma((slots,)),
            dma(()),
            dma(()),
            dma((2 * slots,)),
            dma((2 * slots, 11)),
            dma((5,)),
            dma((2,)),
        ],
        compiler_params=pltpu.CompilerParams(
            collective_id=0, has_side_effects=True, vmem_limit_bytes=105 * 512 * 1024
        ),
        name="shampoo_step",
    )(code, block_slot, grads, stat_left, stat_right, root_left, root_right)


def solution(mesh):
    placed = (
        P(None, "fsdp", "tensor"),
        P(),
        P("fsdp", "tensor", None),
        P("fsdp", "tensor", None),
        P("fsdp", "tensor", None),
        P("fsdp", None, "tensor"),
    )
    return jax.shard_map(
        on_device,
        mesh=mesh,
        in_specs=placed,
        out_specs=(P(None, "fsdp", "tensor"), P("fsdp", "tensor", None), P("fsdp", "tensor", None)),
        check_vma=False,
    )
```
